32 devices in a mesh: gx: 8 (over y, x, core), gy: 4 (over z).
Axes of the slice: x: 2, y: 2, z: 4, core: 2. Of those that a mesh axis runs over, the one named last changes fastest.
Arguments:
- spectra: float32 [16, 4, 33, 4, 512], P('gx', None, None, None, 'gy'), may hold values from 0.05 to 2
- collection: float32 [4, 33, 561], replicated, may hold values from -0.125 to 0.125
- growth_rate: float32 [4, 33], replicated, may hold values from 0.1 to 1
- fall_speed: float32 [4, 33], replicated, may hold values from 0.05 to 0.9
- supersaturation: float32 [16, 4, 512], P('gx', None, 'gy'), may hold values from -0.4 to 0.4
- courant: float32 [16, 4, 512], P('gx', None, 'gy'), may hold values from -0.8 to 0.8
- cloudy: int32 [16, 512], P('gx', 'gy'), may hold values from 0 to 1, as said below
Outputs:
- spectra_out: float32 [16, 4, 33, 4, 512], P('gx', None, None, None, 'gy')
The draws below stay inside these ranges and needn't reach their ends.
Inputs may be any that keep to these rules, and one draw needn't show every extreme that they name: A block is the 128 columns of one x-row that lie on one device; each device holds 2 blocks, and a block is cloudy if any of its entries is 1. In every aligned run of 8 devices along gx with one gy index at most 8 blocks are cloudy; in every draw some run has exactly that many, and some device has all 2 of its blocks cloudy.
All inputs are finite; a program needn't handle non-finite values.
Results may differ from the reference program's by a relative error of at most 0.0003.
Values sent between devices are 32-bit elements; how exact they have to be, the bound alone decides.
A program may use at most 64 MiB of HBM per device.

```python
import math
import jax
import jax.numpy as jnp
from jax import lax

TYPES = 4
BINS = 33
LEV = 4
CY = 128
BLK_DEV = 2
SUB = 2
GROUP = 8
CAP = 1
PAIRS = 561
NX = 16
NY = 512


def draw_cloudy(key, part):
    rows_group = BLK_DEV * GROUP
    x_groups = NX // rows_group
    y_blocks = NY // CY
    group_count = x_groups * y_blocks
    keys = jax.random.split(jax.random.fold_in(key, 7), 6)
    counts = jax.random.randint(keys[0], (group_count,), BLK_DEV, GROUP * CAP + 1)
    full_group = jax.random.randint(keys[1], (), 0, group_count)
    counts = jnp.where(jnp.arange(group_count) == full_group, GROUP * CAP, counts)
    favored = jax.random.randint(keys[2], (group_count, 1), 0, GROUP)
    slot_ids = jnp.arange(rows_group, dtype=jnp.int32)
    scores = jax.random.randint(keys[3], (group_count, rows_group), 0, 1 << 20) * rows_group + slot_ids
    scores = scores + jnp.where(slot_ids[None, :] // BLK_DEV == favored, 1 << 28, 0)
    ordering = jnp.argsort(-scores, axis=1)
    ranking = jnp.argsort(ordering, axis=1)
    block_on = (ranking < counts[:, None]).astype(jnp.int32)
    block_on = block_on.reshape(x_groups, y_blocks, rows_group).transpose(0, 2, 1).reshape(NX, y_blocks, 1)
    column_bits = jax.random.randint(keys[4], (NX, y_blocks, CY), 0, 4) > 0
    forced = jax.random.randint(keys[5], (NX, y_blocks, 1), 0, CY)
    column_on = (column_bits | (jnp.arange(CY)[None, None, :] == forced)).astype(jnp.int32)
    return (block_on * column_on).reshape(NX, NY)


def steps_of(stream_key, dims, cuts, smallest, high):
    loudness = 1.0
    for axis_at, blocks in cuts:
        draws = jax.random.uniform(jax.random.fold_in(jax.random.fold_in(stream_key, 6), axis_at), (blocks,), jnp.float32, smallest / len(cuts), high / len(cuts))
        loudness = loudness * jnp.repeat(jnp.exp(draws), dims[axis_at] // blocks).reshape((-1,) + (1,) * (len(dims) - 1 - axis_at))
    return loudness


def noise(stream_key, extent, deviation, bound, kind=jnp.bfloat16):
    return jnp.clip(deviation * jax.random.normal(stream_key, extent, jnp.float32), -bound, bound).astype(kind)


def setup_inputs(seed: int = 0) -> dict:
    key_list = jax.random.split(jax.random.key(seed), 8)
    spectra = jnp.clip(jnp.exp(math.log(2.0) - 3.6888794 * jax.random.uniform(key_list[0], (NX, TYPES, BINS, LEV, NY), jnp.float32) ** steps_of(key_list[0], (NX, TYPES, BINS, LEV, NY), ((0, 8), (4, 4)), -0.2, 0.2)), 0.05, 2.0)
    collection = noise(key_list[1], (TYPES, BINS, PAIRS), (4 * PAIRS) ** -0.5, 0.125, jnp.float32)
    growth_rate = jnp.clip(jnp.exp(jax.random.uniform(key_list[2], (TYPES, BINS), jnp.float32, math.log(0.1), math.log(1.0))), 0.1, 1.0)
    fall_speed = jnp.clip(jnp.exp(jax.random.uniform(key_list[3], (TYPES, BINS), jnp.float32, math.log(0.05), math.log(0.9))), 0.05, 0.9)
    supersaturation = jnp.clip(jax.random.uniform(key_list[4], (NX, LEV, NY), jnp.float32, -0.4, 0.4) * steps_of(key_list[4], (NX, LEV, NY), ((0, 8), (2, 4)), -0.4, 0.0), -0.4, 0.4)
    courant = jnp.clip(jax.random.uniform(key_list[5], (NX, LEV, NY), jnp.float32, -0.8, 0.8) * steps_of(key_list[5], (NX, LEV, NY), ((0, 8), (2, 4)), -0.4, 0.0), -0.8, 0.8)
    cloudy = draw_cloudy(jax.random.fold_in(key_list[7], 71), 0)
    return {"spectra": spectra, "collection": collection, "growth_rate": growth_rate, "fall_speed": fall_speed, "supersaturation": supersaturation, "courant": courant, "cloudy": cloudy}


precise_mode = lax.Precision.HIGHEST


def pair_products(matrix):
    pieces = [matrix[first:first + 1] * matrix[first:] for first in range(matrix.shape[0])]
    return jnp.concatenate(pieces, axis=0)


def condense(block, saturation, growth_rate):
    rising = jnp.maximum(saturation, 0.0)
    falling = jnp.maximum(-saturation, 0.0)
    transfer = growth_rate[:, :, None, None] * block
    upward = rising * transfer
    upward = jnp.concatenate([upward[:, :-1], jnp.zeros_like(upward[:, :1])], axis=1)
    downward = falling * transfer
    arrive_up = jnp.concatenate([jnp.zeros_like(upward[:, :1]), upward[:, :-1]], axis=1)
    arrive_down = jnp.concatenate([downward[:, 1:], jnp.zeros_like(downward[:, :1])], axis=1)
    return block - upward - downward + arrive_up + arrive_down


def collide(block, collection):
    results = []
    for species in range(block.shape[0]):
        matrix = block[species].reshape(block.shape[1], -1)
        gained = jnp.dot(collection[species], pair_products(matrix), precision=precise_mode, preferred_element_type=jnp.float32)
        results.append(matrix + gained)
    return jnp.stack(results).reshape(block.shape)


def micro_block(block, saturation, cloudy_row, growth_rate, collection):
    grown = condense(block, saturation, growth_rate)
    for substep in range(SUB):
        grown = collide(grown, collection)
    return jnp.where(cloudy_row > 0, grown, block)


def sediment(block, fall_speed):
    above = jnp.concatenate([block[..., 1:, :], jnp.zeros_like(block[..., :1, :])], axis=-2)
    return block + fall_speed[:, :, None, None] * (above - block)


def advect(extended, courant_ext):
    columns = extended.shape[-1] - 4
    face_courant = 0.5 * (courant_ext[..., 1:columns + 2] + courant_ext[..., 2:columns + 3])
    minus_one = extended[..., 0:columns + 1]
    centre = extended[..., 1:columns + 2]
    plus_one = extended[..., 2:columns + 3]
    plus_two = extended[..., 3:columns + 4]
    central = (7.0 * (plus_one + centre) - (plus_two + minus_one)) / 12.0
    upwind = ((plus_two - minus_one) - 3.0 * (plus_one - centre)) / 12.0
    fluxes = face_courant * central - jnp.abs(face_courant) * upwind
    return extended[..., 2:columns + 2] - (fluxes[..., 1:] - fluxes[..., :-1])


def reference(spectra, collection, growth_rate, fall_speed, supersaturation, courant, cloudy):
    def one_row(pieces):
        block, saturation, wind_row, cloudy_row = pieces
        wetted = micro_block(block, saturation, cloudy_row, growth_rate, collection)
        settled = sediment(wetted, fall_speed)
        extended = jnp.concatenate([settled[..., -2:], settled, settled[..., :2]], axis=-1)
        wind_ext = jnp.concatenate([wind_row[..., -2:], wind_row, wind_row[..., :2]], axis=-1)
        return advect(extended, wind_ext)
    return lax.map(one_row, (spectra, supersaturation, courant, cloudy))
```

```python
import functools

import jax
import jax.numpy as jnp
from jax import lax
from jax.experimental import pallas as pl
from jax.experimental.pallas import tpu as pltpu
from jax.sharding import PartitionSpec as P

SUB = 2
LANES = 128
CHUNK = 4
F32 = jnp.float32
BF16 = jnp.bfloat16


def rounded(x):
    return x.astype(BF16).astype(F32)


def kernel(
    dims,
    f_ref,
    coll_ref,
    rate_ref,
    fall_ref,
    sat_ref,
    cour_ref,
    cloudy_ref,
    out_ref,
    cm,
    k_last,
    tail,
    cells,
    gs,
    edge,
    from_left,
    from_right,
    send_sem,
    recv_sem,
):
    blocks, types, bins, levels, cols, n_y = dims
    low = bins // 8 * 8
    rows = low + 8
    per_type = blocks * levels
    groups = types * per_type
    me = lax.axis_index("gy")
    right, left = lax.rem(me + 1, n_y), lax.rem(me + n_y - 1, n_y)
    mesh_id = pl.DeviceIdType.MESH
    barrier = pltpu.get_barrier_semaphore()
    for peer in (left, right):
        pl.semaphore_signal(barrier, inc=1, device_id={"gy": peer}, device_id_type=mesh_id)

    lane = lax.broadcasted_iota(jnp.int32, (rows, LANES), 1)
    sub = lax.broadcasted_iota(jnp.int32, (rows, LANES), 0)

    edge[...] = jnp.zeros_like(edge)
    for t in range(types):
        for b in range(blocks):
            for v in range(levels):
                g = (t * blocks + b) * levels + v
                base = ((b * types + t) * bins) * levels + v
                cells[g, bins:rows] = jnp.zeros((rows - bins, cols), F32)
                cells[g, 0:bins] = f_ref[pl.ds(base, bins, stride=levels), :]
                cells[g, bins : bins + 1] = cour_ref[b, v : v + 1, :]
                cells[g, bins + 1 : bins + 2] = sat_ref[b, v : v + 1, :]
                cells[g, bins + 2 : bins + 3] = cloudy_ref[b : b + 1, :].astype(F32)
    packed = jnp.zeros((rows, LANES), F32)
    for g in range(groups):
        packed = jnp.where(
            (lane >= 4 * g) & (lane < 4 * g + 4),
            pltpu.roll(cells[g], (4 * g + 2) % LANES, 1),
            packed,
        )
    edge[...] = packed

    pl.semaphore_wait(barrier, 2)
    copies = []
    for index, (peer, landing) in enumerate(((right, from_left), (left, from_right))):
        copy = pltpu.make_async_remote_copy(
            src_ref=edge,
            dst_ref=landing,
            send_sem=send_sem.at[index],
            recv_sem=recv_sem.at[index],
            device_id={"gy": peer},
            device_id_type=mesh_id,
        )
        copy.start()
        copies.append(copy)

    def column(ref, t):
        row = jnp.broadcast_to(ref[t : t + 1, :], (rows, bins))
        r = lax.broadcasted_iota(jnp.int32, (rows, bins), 0)
        c = lax.broadcasted_iota(jnp.int32, (rows, bins), 1)
        return jnp.sum(jnp.where(r == c, row, 0.0), axis=1, keepdims=True)

    rates = [jnp.broadcast_to(column(rate_ref, t), (rows, LANES)) for t in range(types)]
    falls = [jnp.broadcast_to(column(fall_ref, t), (rows, LANES)) for t in range(types)]

    pairs = coll_ref.shape[2]
    whole = pairs // LANES
    lane_b = lax.broadcasted_iota(jnp.int32, (bins, LANES), 1)
    for t in range(types):
        tail[...] = jnp.zeros_like(tail)
        if pairs % LANES:
            tail[0:bins, 0 : pairs - whole * LANES] = coll_ref[t, :, whole * LANES : pairs]
        k_last[...] = jnp.zeros_like(k_last)

        def tile(a):
            if a < whole:
                return coll_ref[t, :, a * LANES : (a + 1) * LANES]
            return tail[0:bins]

        first = 0
        for i in range(bins):
            count = bins - i
            a, end = first // LANES, (first + count - 1) // LANES
            shift = (i - first) % LANES
            x = pltpu.roll(tile(a), shift, 1) if shift else tile(a)
            if end > a:
                split = i + (a + 1) * LANES - first
                y = pltpu.roll(tile(end), shift, 1) if shift else tile(end)
                x = jnp.where(lane_b < split, x, y)
            x = jnp.where((lane_b >= i) & (lane_b < bins), x, 0.0)
            hi = rounded(x)
            stack = hi + pltpu.roll(x - hi, rows, 1) + pltpu.roll(hi, 2 * rows, 1)
            cm[t, i * low : (i + 1) * low] = stack[0:low].astype(BF16)
            k_last[i : i + 1] = stack[low:bins]
            first += count
        cm[t, bins * low :] = k_last[...].astype(BF16)

    def condense(f, r, sat):
        fr = r * f
        top = lax.broadcasted_iota(jnp.int32, f.shape, 0) < bins - 1
        up = jnp.where(top, fr, 0.0)
        rise = pltpu.roll(up, 1, 0) - up
        fall = pltpu.roll(fr, rows - 1, 0) - fr
        return f + jnp.maximum(sat, 0.0) * rise + jnp.maximum(-sat, 0.0) * fall

    def collide(t, g):
        width = g.shape[1]
        slot = gs.at[:, 0:width]
        slot[...] = g
        hi = rounded(g)
        stack = jnp.concatenate(
            [hi, hi, g - hi, jnp.zeros((LANES - 3 * rows, width), F32)], axis=0
        ).astype(BF16)
        acc = g[0:low]
        for start in range(0, bins, CHUNK):
            stop = min(start + CHUNK, bins)
            h = jnp.dot(cm[t, start * low : stop * low], stack, preferred_element_type=F32)
            for i in range(start, stop):
                acc = acc + slot[i : i + 1, :] * h[(i - start) * low : (i - start + 1) * low]
        h = jnp.dot(cm[t, bins * low :], stack, preferred_element_type=F32)
        last = jnp.sum(g * h[0:rows], axis=0, keepdims=True)
        rest = g[low:rows]
        rest = jnp.where(lax.broadcasted_iota(jnp.int32, rest.shape, 0) == 0, rest + last, rest)
        return jnp.concatenate([acc, rest], axis=0)

    def two(x, times):
        return jnp.concatenate([x] * times, axis=1) if times > 1 else x

    per = 2 if levels % 2 == 0 else 1
    for t in range(types):

        def one_block(b, carry, t=t):
            base = (t * blocks + b) * levels
            wet = []
            for v in range(0, levels, per):
                f = jnp.concatenate([cells[base + v + p] for p in range(per)], axis=1)
                g = condense(f, two(rates[t], per), f[bins + 1 : bins + 2])
                for _ in range(SUB):
                    g = collide(t, g)
                w = jnp.where(f[bins + 2 : bins + 3] > 0, g, f)
                wet += [w[:, p * LANES : (p + 1) * LANES] for p in range(per)]
            for v in range(levels):
                above = wet[v + 1] if v + 1 < levels else jnp.zeros_like(wet[v])
                cells[base + v] = wet[v] + falls[t] * (above - wet[v])
            return carry

        lax.fori_loop(0, blocks, one_block, 0)

    for copy in copies:
        copy.wait()
    f = jnp.where(lane % 4 < 2, from_left[...], from_right[...])
    kind = lane // (4 * per_type)
    r, v_fall = rates[0], falls[0]
    for t in range(1, types):
        r = jnp.where(kind == t, rates[t], r)
        v_fall = jnp.where(kind == t, falls[t], v_fall)
    g = condense(f, r, f[bins + 1 : bins + 2])
    for _ in range(SUB):
        new = collide(0, g)
        for t in range(1, types):
            new = jnp.where(kind == t, collide(t, g), new)
        g = new
    w = jnp.where(f[bins + 2 : bins + 3] > 0, g, f)
    above = jnp.where(lane // 4 % levels == levels - 1, 0.0, pltpu.roll(w, LANES - 4, 1))
    ghost = w + v_fall * (above - w)
    edge[...] = ghost

    def shifted(g, x, width_lane):
        near = pltpu.roll(edge[...], (cols - 2 - 4 * g) % LANES, 1)
        m2 = pltpu.roll(jnp.where(width_lane >= cols - 2, near, x), 2, 1)
        m1 = pltpu.roll(jnp.where(width_lane == cols - 1, near, x), 1, 1)
        p1 = pltpu.roll(jnp.where(width_lane == 0, near, x), LANES - 1, 1)
        p2 = pltpu.roll(jnp.where(width_lane < 2, near, x), LANES - 2, 1)
        return m2, m1, p1, p2

    for b in range(blocks):
        for v in range(levels):
            coef = None
            for t in range(types):
                g = (t * blocks + b) * levels + v
                x = cells[g]
                m2, m1, p1, p2 = shifted(g, x, lane)
                if coef is None:
                    c = 0.5 * (x[bins : bins + 1] + p1[bins : bins + 1])
                    d = 0.5 * (x[bins : bins + 1] + m1[bins : bins + 1])
                    ca, da = jnp.abs(c), jnp.abs(d)
                    coef = [
                        jnp.broadcast_to(e * (1.0 / 12.0), (rows, LANES))
                        for e in (
                            da - d,
                            7.0 * d - 3.0 * da - (ca - c),
                            7.0 * d + 3.0 * da - (7.0 * c - 3.0 * ca),
                            -d - da - (7.0 * c + 3.0 * ca),
                            c + ca,
                        )
                    ]
                y = x + coef[2] * x + coef[0] * m2 + coef[1] * m1 + coef[3] * p1 + coef[4] * p2
                base = ((b * types + t) * bins) * levels + v
                out_ref[pl.ds(base, bins, stride=levels), :] = y[0:bins]


def body(n_y, spectra, collection, growth_rate, fall_speed, supersaturation, courant, cloudy):
    blocks, types, bins, levels, cols = spectra.shape
    dims = (blocks, types, bins, levels, cols, n_y)
    low = bins // 8 * 8
    rows = low + 8
    total = blocks * types * bins * levels
    last = -(-rows // 16) * 16
    vmem = pl.BlockSpec(memory_space=pltpu.VMEM)
    out = pl.pallas_call(
        functools.partial(kernel, dims),
        out_shape=jax.ShapeDtypeStruct((total, cols), F32),
        in_specs=[vmem] * 7,
        out_specs=vmem,
        scratch_shapes=[
            pltpu.VMEM((types, bins * low + last, LANES), BF16),
            pltpu.VMEM((last, LANES), F32),
            pltpu.VMEM((rows, LANES), F32),
            pltpu.VMEM((blocks * types * levels, rows, cols), F32),
            pltpu.VMEM((rows, 2 * cols), F32),
            pltpu.VMEM((rows, LANES), F32),
            pltpu.VMEM((rows, LANES), F32),
            pltpu.VMEM((rows, LANES), F32),
            pltpu.SemaphoreType.DMA((2,)),
            pltpu.SemaphoreType.DMA((2,)),
        ],
        compiler_params=pltpu.CompilerParams(
            collective_id=0, has_side_effects=True, vmem_limit_bytes=32 * 2**20
        ),
    )(
        spectra.reshape(total, cols),
        collection,
        growth_rate,
        fall_speed,
        supersaturation,
        courant,
        cloudy,
    )
    return out.reshape(spectra.shape)


def solution(mesh):
    return jax.shard_map(
        functools.partial(body, mesh.shape["gy"]),
        mesh=mesh,
        in_specs=(
            P("gx", None, None, None, "gy"),
            P(),
            P(),
            P(),
            P("gx", None, "gy"),
            P("gx", None, "gy"),
            P("gx", "gy"),
        ),
        out_specs=P("gx", None, None, None, "gy"),
        check_vma=False,
    )
```

```python
import functools

import jax
import jax.numpy as jnp
from jax import lax
from jax.experimental import pallas as pl
from jax.experimental.pallas import tpu as pltpu
from jax.sharding import PartitionSpec as P

SUB = 2
LANES = 128
CHUNK = 4
F32 = jnp.float32
BF16 = jnp.bfloat16


def rounded(x):
    return x.astype(BF16).astype(F32)


def kernel(
    dims,
    f_ref,
    coll_ref,
    rate_ref,
    fall_ref,
    sat_ref,
    cour_ref,
    cloudy_ref,
    out_ref,
    cm,
    k_last,
    tail,
    cells,
    gs,
    rates,
    falls,
    edge,
    from_left,
    from_right,
    send_sem,
    recv_sem,
):
    blocks, types, bins, levels, cols, n_y = dims
    low = bins // 8 * 8
    rows = low + 8
    per_type = blocks * levels
    groups = types * per_type
    me = lax.axis_index("gy")
    right, left = lax.rem(me + 1, n_y), lax.rem(me + n_y - 1, n_y)
    mesh_id = pl.DeviceIdType.MESH
    barrier = pltpu.get_barrier_semaphore()
    for peer in (left, right):
        pl.semaphore_signal(barrier, inc=1, device_id={"gy": peer}, device_id_type=mesh_id)

    lane = lax.broadcasted_iota(jnp.int32, (rows, LANES), 1)
    sub = lax.broadcasted_iota(jnp.int32, (rows, LANES), 0)

    def fill(t, packed):
        for b in range(blocks):
            for v in range(levels):
                g = (t * blocks + b) * levels + v
                base = ((b * types + t) * bins) * levels + v
                cells[g, bins:rows] = jnp.zeros((rows - bins, cols), F32)
                cells[g, 0:bins] = f_ref[pl.ds(base, bins, stride=levels), :]
                cells[g, bins : bins + 1] = cour_ref[b, v : v + 1, :]
                cells[g, bins + 1 : bins + 2] = sat_ref[b, v : v + 1, :]
                cells[g, bins + 2 : bins + 3] = cloudy_ref[b : b + 1, :].astype(F32)
                turned = pltpu.roll(cells[g], lax.rem(4 * g + 2, LANES), 1)
                packed = jnp.where((lane >= 4 * g) & (lane < 4 * g + 4), turned, packed)
        return packed

    packed = lax.fori_loop(0, types, fill, jnp.zeros((rows, LANES), F32))
    edge[...] = packed

    pl.semaphore_wait(barrier, 2)
    copies = []
    for index, (peer, landing) in enumerate(((right, from_left), (left, from_right))):
        copy = pltpu.make_async_remote_copy(
            src_ref=edge,
            dst_ref=landing,
            send_sem=send_sem.at[index],
            recv_sem=recv_sem.at[index],
            device_id={"gy": peer},
            device_id_type=mesh_id,
        )
        copy.start()
        copies.append(copy)

    def column(ref, t):
        row = jnp.broadcast_to(ref[t : t + 1, :], (rows, bins))
        r = lax.broadcasted_iota(jnp.int32, (rows, bins), 0)
        c = lax.broadcasted_iota(jnp.int32, (rows, bins), 1)
        return jnp.sum(jnp.where(r == c, row, 0.0), axis=1, keepdims=True)

    for t in range(types):
        rates[t] = jnp.broadcast_to(column(rate_ref, t), (rows, LANES))
        falls[t] = jnp.broadcast_to(column(fall_ref, t), (rows, LANES))

    pairs = coll_ref.shape[2]
    whole = pairs // LANES
    lane_b = lax.broadcasted_iota(jnp.int32, (bins, LANES), 1)

    def coefficients(t, carry):
        tail[...] = jnp.zeros_like(tail)
        if pairs % LANES:
            tail[0:bins, 0 : pairs - whole * LANES] = coll_ref[t, :, whole * LANES : pairs]
        k_last[...] = jnp.zeros_like(k_last)

        def tile(a):
            if a < whole:
                return coll_ref[t, :, a * LANES : (a + 1) * LANES]
            return tail[0:bins]

        first = 0
        for i in range(bins):
            count = bins - i
            a, end = first // LANES, (first + count - 1) // LANES
            shift = (i - first) % LANES
            x = pltpu.roll(tile(a), shift, 1) if shift else tile(a)
            if end > a:
                split = i + (a + 1) * LANES - first
                y = pltpu.roll(tile(end), shift, 1) if shift else tile(end)
                x = jnp.where(lane_b < split, x, y)
            x = jnp.where((lane_b >= i) & (lane_b < bins), x, 0.0)
            hi = rounded(x)
            stack = hi + pltpu.roll(x - hi, rows, 1) + pltpu.roll(hi, 2 * rows, 1)
            cm[t, i * low : (i + 1) * low] = stack[0:low].astype(BF16)
            k_last[i : i + 1] = stack[low:bins]
            first += count
        cm[t, bins * low :] = k_last[...].astype(BF16)
        return carry

    lax.fori_loop(0, types, coefficients, 0)

    def condense(f, r, sat):
        fr = r * f
        top = lax.broadcasted_iota(jnp.int32, f.shape, 0) < bins - 1
        up = jnp.where(top, fr, 0.0)
        rise = pltpu.roll(up, 1, 0) - up
        fall = pltpu.roll(fr, rows - 1, 0) - fr
        return f + jnp.maximum(sat, 0.0) * rise + jnp.maximum(-sat, 0.0) * fall

    def collide(t, g):
        width = g.shape[1]
        slot = gs.at[:, 0:width]
        slot[...] = g
        hi = rounded(g)
        stack = jnp.concatenate(
            [hi, hi, g - hi, jnp.zeros((LANES - 3 * rows, width), F32)], axis=0
        ).astype(BF16)
        acc = g[0:low]
        for start in range(0, bins, CHUNK):
            stop = min(start + CHUNK, bins)
            h = jnp.dot(cm[t, start * low : stop * low], stack, preferred_element_type=F32)
            for i in range(start, stop):
                acc = acc + slot[i : i + 1, :] * h[(i - start) * low : (i - start + 1) * low]
        h = jnp.dot(cm[t, bins * low :], stack, preferred_element_type=F32)
        last = jnp.sum(g * h[0:rows], axis=0, keepdims=True)
        rest = g[low:rows]
        rest = jnp.where(lax.broadcasted_iota(jnp.int32, rest.shape, 0) == 0, rest + last, rest)
        return jnp.concatenate([acc, rest], axis=0)

    def two(x, times):
        return jnp.concatenate([x] * times, axis=1) if times > 1 else x

    per = 2 if levels % 2 == 0 else 1

    def one_block(at, carry):
        t, base = at // blocks, at * levels
        wet = []
        for v in range(0, levels, per):
            f = jnp.concatenate([cells[base + v + p] for p in range(per)], axis=1)
            g = condense(f, two(rates[t], per), f[bins + 1 : bins + 2])
            for _ in range(SUB):
                g = collide(t, g)
            w = jnp.where(f[bins + 2 : bins + 3] > 0, g, f)
            wet += [w[:, p * LANES : (p + 1) * LANES] for p in range(per)]
        for v in range(levels):
            above = wet[v + 1] if v + 1 < levels else jnp.zeros_like(wet[v])
            cells[base + v] = wet[v] + falls[t] * (above - wet[v])
        return carry

    lax.fori_loop(0, types * blocks, one_block, 0)

    for copy in copies:
        copy.wait()
    f = jnp.where(lane % 4 < 2, from_left[...], from_right[...])
    kind = lane // (4 * per_type)
    r, v_fall = rates[0], falls[0]
    for t in range(1, types):
        r = jnp.where(kind == t, rates[t], r)
        v_fall = jnp.where(kind == t, falls[t], v_fall)
    g = condense(f, r, f[bins + 1 : bins + 2])

    def one_type(t, new):
        mine = g
        for _ in range(SUB):
            mine = collide(t, mine)
        return jnp.where(kind == t, mine, new)

    g = lax.fori_loop(0, types, one_type, g)
    w = jnp.where(f[bins + 2 : bins + 3] > 0, g, f)
    above = jnp.where(lane // 4 % levels == levels - 1, 0.0, pltpu.roll(w, LANES - 4, 1))
    ghost = w + v_fall * (above - w)
    edge[...] = ghost

    def shifted(g, x, width_lane):
        near = pltpu.roll(edge[...], lax.rem(cols + LANES - 2 - 4 * g, LANES), 1)
        m2 = pltpu.roll(jnp.where(width_lane >= cols - 2, near, x), 2, 1)
        m1 = pltpu.roll(jnp.where(width_lane == cols - 1, near, x), 1, 1)
        p1 = pltpu.roll(jnp.where(width_lane == 0, near, x), LANES - 1, 1)
        p2 = pltpu.roll(jnp.where(width_lane < 2, near, x), LANES - 2, 1)
        return m2, m1, p1, p2

    def advect(at, carry):
        b, v = at // levels, lax.rem(at, levels)
        coef = None
        for t in range(types):
            g = (t * blocks + b) * levels + v
            x = cells[g]
            m2, m1, p1, p2 = shifted(g, x, lane)
            if coef is None:
                c = 0.5 * (x[bins : bins + 1] + p1[bins : bins + 1])
                d = 0.5 * (x[bins : bins + 1] + m1[bins : bins + 1])
                ca, da = jnp.abs(c), jnp.abs(d)
                coef = [
                    jnp.broadcast_to(e * (1.0 / 12.0), (rows, LANES))
                    for e in (
                        da - d,
                        7.0 * d - 3.0 * da - (ca - c),
                        7.0 * d + 3.0 * da - (7.0 * c - 3.0 * ca),
                        -d - da - (7.0 * c + 3.0 * ca),
                        c + ca,
                    )
                ]
            y = x + coef[2] * x + coef[0] * m2 + coef[1] * m1 + coef[3] * p1 + coef[4] * p2
            base = ((b * types + t) * bins) * levels + v
            out_ref[pl.ds(base, bins, stride=levels), :] = y[0:bins]
        return carry

    lax.fori_loop(0, per_type, advect, 0)


def body(n_y, spectra, collection, growth_rate, fall_speed, supersaturation, courant, cloudy):
    blocks, types, bins, levels, cols = spectra.shape
    dims = (blocks, types, bins, levels, cols, n_y)
    low = bins // 8 * 8
    rows = low + 8
    total = blocks * types * bins * levels
    last = -(-rows // 16) * 16
    vmem = pl.BlockSpec(memory_space=pltpu.VMEM)
    out = pl.pallas_call(
        functools.partial(kernel, dims),
        out_shape=jax.ShapeDtypeStruct((total, cols), F32),
        in_specs=[vmem] * 7,
        out_specs=vmem,
        scratch_shapes=[
            pltpu.VMEM((types, bins * low + last, LANES), BF16),
            pltpu.VMEM((last, LANES), F32),
            pltpu.VMEM((rows, LANES), F32),
            pltpu.VMEM((blocks * types * levels, rows, cols), F32),
            pltpu.VMEM((rows, 2 * cols), F32),
            pltpu.VMEM((types, rows, LANES), F32),
            pltpu.VMEM((types, rows, LANES), F32),
            pltpu.VMEM((rows, LANES), F32),
            pltpu.VMEM((rows, LANES), F32),
            pltpu.VMEM((rows, LANES), F32),
            pltpu.SemaphoreType.DMA((2,)),
            pltpu.SemaphoreType.DMA((2,)),
        ],
        compiler_params=pltpu.CompilerParams(
            collective_id=0, has_side_effects=True, vmem_limit_bytes=32 * 2**20
        ),
    )(
        spectra.reshape(total, cols),
        collection,
        growth_rate,
        fall_speed,
        supersaturation,
        courant,
        cloudy,
    )
    return out.reshape(spectra.shape)


def solution(mesh):
    return jax.shard_map(
        functools.partial(body, mesh.shape["gy"]),
        mesh=mesh,
        in_specs=(
            P("gx", None, None, None, "gy"),
            P(),
            P(),
            P(),
            P("gx", None, "gy"),
            P("gx", None, "gy"),
            P("gx", "gy"),
        ),
        out_specs=P("gx", None, None, None, "gy"),
        check_vma=False,
    )
```

```python
import functools

import jax
import jax.numpy as jnp
from jax import lax
from jax.experimental import pallas as pl
from jax.experimental.pallas import tpu as pltpu
from jax.sharding import PartitionSpec as P

SUB = 2
LANES = 128
CHUNK = 4
F32 = jnp.float32
BF16 = jnp.bfloat16


def rounded(x):
    return x.astype(BF16).astype(F32)


def kernel(
    dims,
    f_ref,
    coll_ref,
    rate_ref,
    fall_ref,
    sat_ref,
    cour_ref,
    cloudy_ref,
    out_ref,
    cm,
    k_last,
    raw,
    cells,
    gs,
    rates,
    falls,
    edge,
    from_left,
    from_right,
    send_sem,
    recv_sem,
):
    blocks, types, bins, levels, cols, n_y = dims
    low = bins // 8 * 8
    rows = low + 8
    per_type = blocks * levels
    groups = types * per_type
    me = lax.axis_index("gy")
    right, left = lax.rem(me + 1, n_y), lax.rem(me + n_y - 1, n_y)
    mesh_id = pl.DeviceIdType.MESH
    barrier = pltpu.get_barrier_semaphore()
    for peer in (left, right):
        pl.semaphore_signal(barrier, inc=1, device_id={"gy": peer}, device_id_type=mesh_id)

    lane = lax.broadcasted_iota(jnp.int32, (rows, LANES), 1)
    sub = lax.broadcasted_iota(jnp.int32, (rows, LANES), 0)

    def fill(t, packed):
        for b in range(blocks):
            for v in range(levels):
                g = (t * blocks + b) * levels + v
                base = ((b * types + t) * bins) * levels + v
                cells[g, bins:rows] = jnp.zeros((rows - bins, cols), F32)
                cells[g, 0:bins] = f_ref[pl.ds(base, bins, stride=levels), :]
                cells[g, bins : bins + 1] = cour_ref[b, v : v + 1, :]
                cells[g, bins + 1 : bins + 2] = sat_ref[b, v : v + 1, :]
                cells[g, bins + 2 : bins + 3] = cloudy_ref[b : b + 1, :].astype(F32)
                turned = pltpu.roll(cells[g], lax.rem(4 * g + 2, LANES), 1)
                packed = jnp.where((lane >= 4 * g) & (lane < 4 * g + 4), turned, packed)
        return packed

    packed = lax.fori_loop(0, types, fill, jnp.zeros((rows, LANES), F32))
    edge[...] = packed

    def column(ref, t):
        row = jnp.broadcast_to(ref[t : t + 1, :], (rows, bins))
        r = lax.broadcasted_iota(jnp.int32, (rows, bins), 0)
        c = lax.broadcasted_iota(jnp.int32, (rows, bins), 1)
        return jnp.sum(jnp.where(r == c, row, 0.0), axis=1, keepdims=True)

    for t in range(types):
        rates[t] = jnp.broadcast_to(column(rate_ref, t), (rows, LANES))
        falls[t] = jnp.broadcast_to(column(fall_ref, t), (rows, LANES))

    pairs = coll_ref.shape[2]
    raw[...] = jnp.zeros_like(raw)
    k_last[...] = jnp.zeros_like(k_last)
    sources = []
    for a in range(raw.shape[0]):
        width = min(LANES, pairs - a * LANES)
        for t in range(types):
            raw[a, t * rows : t * rows + bins, 0:width] = coll_ref[t, :, a * LANES : a * LANES + width]
        x = raw[a]
        hi = x.astype(BF16)
        sources.append(jnp.concatenate([hi, (x - hi.astype(F32)).astype(BF16)], axis=1))
    across = lax.broadcasted_iota(jnp.int32, (LANES, LANES), 1)
    down = lax.broadcasted_iota(jnp.int32, (LANES, LANES), 0)
    part, inner = across // rows, across % rows
    inner = jnp.where(inner < bins, inner, -1)
    inner_hi = jnp.where((part == 0) | (part == 2), inner, -1)
    inner_lo = jnp.where(part == 1, inner, -1)
    first = 0
    for i in range(bins):
        placed = None
        for a in range(first // LANES, (first + bins - i - 1) // LANES + 1):
            offset = first - i - a * LANES
            pick = jnp.concatenate(
                [
                    jnp.where((down == j + offset) & (j >= i), 1.0, 0.0).astype(BF16)
                    for j in (inner_hi, inner_lo)
                ],
                axis=0,
            )
            product = jnp.dot(sources[a], pick, preferred_element_type=F32)
            placed = product if placed is None else placed + product
        for t in range(types):
            cm[t, i * low : (i + 1) * low] = placed[t * rows : t * rows + low].astype(BF16)
            k_last[t, i : i + 1] = placed[t * rows + low : t * rows + bins]
        first += bins - i
    for t in range(types):
        cm[t, bins * low :] = k_last[t].astype(BF16)

    pl.semaphore_wait(barrier, 2)
    copies = []
    for index, (peer, landing) in enumerate(((right, from_left), (left, from_right))):
        copy = pltpu.make_async_remote_copy(
            src_ref=edge,
            dst_ref=landing,
            send_sem=send_sem.at[index],
            recv_sem=recv_sem.at[index],
            device_id={"gy": peer},
            device_id_type=mesh_id,
        )
        copy.start()
        copies.append(copy)

    def condense(f, r, sat):
        fr = r * f
        top = lax.broadcasted_iota(jnp.int32, f.shape, 0) < bins - 1
        up = jnp.where(top, fr, 0.0)
        rise = pltpu.roll(up, 1, 0) - up
        fall = pltpu.roll(fr, rows - 1, 0) - fr
        return f + jnp.maximum(sat, 0.0) * rise + jnp.maximum(-sat, 0.0) * fall

    def collide(t, g):
        width = g.shape[1]
        slot = gs.at[:, 0:width]
        slot[...] = g
        hi = rounded(g)
        stack = jnp.concatenate(
            [hi, hi, g - hi, jnp.zeros((LANES - 3 * rows, width), F32)], axis=0
        ).astype(BF16)
        acc = g[0:low]
        for start in range(0, bins, CHUNK):
            stop = min(start + CHUNK, bins)
            h = jnp.dot(cm[t, start * low : stop * low], stack, preferred_element_type=F32)
            for i in range(start, stop):
                acc = acc + slot[i : i + 1, :] * h[(i - start) * low : (i - start + 1) * low]
        h = jnp.dot(cm[t, bins * low :], stack, preferred_element_type=F32)
        last = jnp.sum(g * h[0:rows], axis=0, keepdims=True)
        rest = g[low:rows]
        rest = jnp.where(lax.broadcasted_iota(jnp.int32, rest.shape, 0) == 0, rest + last, rest)
        return jnp.concatenate([acc, rest], axis=0)

    def two(x, times):
        return jnp.concatenate([x] * times, axis=1) if times > 1 else x

    per = 2 if levels % 2 == 0 else 1

    def one_block(at, carry):
        t, base = at // blocks, at * levels
        wet = []
        for v in range(0, levels, per):
            f = jnp.concatenate([cells[base + v + p] for p in range(per)], axis=1)
            g = condense(f, two(rates[t], per), f[bins + 1 : bins + 2])
            for _ in range(SUB):
                g = collide(t, g)
            w = jnp.where(f[bins + 2 : bins + 3] > 0, g, f)
            wet += [w[:, p * LANES : (p + 1) * LANES] for p in range(per)]
        for v in range(levels):
            above = wet[v + 1] if v + 1 < levels else jnp.zeros_like(wet[v])
            cells[base + v] = wet[v] + falls[t] * (above - wet[v])
        return carry

    lax.fori_loop(0, types * blocks, one_block, 0)

    for copy in copies:
        copy.wait()
    f = jnp.where(lane % 4 < 2, from_left[...], from_right[...])
    kind = lane // (4 * per_type)
    r, v_fall = rates[0], falls[0]
    for t in range(1, types):
        r = jnp.where(kind == t, rates[t], r)
        v_fall = jnp.where(kind == t, falls[t], v_fall)
    g = condense(f, r, f[bins + 1 : bins + 2])

    def one_type(t, new):
        mine = g
        for _ in range(SUB):
            mine = collide(t, mine)
        return jnp.where(kind == t, mine, new)

    g = lax.fori_loop(0, types, one_type, g)
    w = jnp.where(f[bins + 2 : bins + 3] > 0, g, f)
    above = jnp.where(lane // 4 % levels == levels - 1, 0.0, pltpu.roll(w, LANES - 4, 1))
    ghost = w + v_fall * (above - w)
    edge[...] = ghost

    def shifted(g, x, width_lane):
        near = pltpu.roll(edge[...], lax.rem(cols + LANES - 2 - 4 * g, LANES), 1)
        m2 = pltpu.roll(jnp.where(width_lane >= cols - 2, near, x), 2, 1)
        m1 = pltpu.roll(jnp.where(width_lane == cols - 1, near, x), 1, 1)
        p1 = pltpu.roll(jnp.where(width_lane == 0, near, x), LANES - 1, 1)
        p2 = pltpu.roll(jnp.where(width_lane < 2, near, x), LANES - 2, 1)
        return m2, m1, p1, p2

    def advect(at, carry):
        b, v = at // levels, lax.rem(at, levels)
        coef = None
        for t in range(types):
            g = (t * blocks + b) * levels + v
            x = cells[g]
            m2, m1, p1, p2 = shifted(g, x, lane)
            if coef is None:
                c = 0.5 * (x[bins : bins + 1] + p1[bins : bins + 1])
                d = 0.5 * (x[bins : bins + 1] + m1[bins : bins + 1])
                ca, da = jnp.abs(c), jnp.abs(d)
                coef = [
                    jnp.broadcast_to(e * (1.0 / 12.0), (rows, LANES))
                    for e in (
                        da - d,
                        7.0 * d - 3.0 * da - (ca - c),
                        7.0 * d + 3.0 * da - (7.0 * c - 3.0 * ca),
                        -d - da - (7.0 * c + 3.0 * ca),
                        c + ca,
                    )
                ]
            y = x + coef[2] * x + coef[0] * m2 + coef[1] * m1 + coef[3] * p1 + coef[4] * p2
            base = ((b * types + t) * bins) * levels + v
            out_ref[pl.ds(base, bins, stride=levels), :] = y[0:bins]
        return carry

    lax.fori_loop(0, per_type, advect, 0)


def body(n_y, spectra, collection, growth_rate, fall_speed, supersaturation, courant, cloudy):
    blocks, types, bins, levels, cols = spectra.shape
    dims = (blocks, types, bins, levels, cols, n_y)
    low = bins // 8 * 8
    rows = low + 8
    total = blocks * types * bins * levels
    last = -(-rows // 16) * 16
    vmem = pl.BlockSpec(memory_space=pltpu.VMEM)
    out = pl.pallas_call(
        functools.partial(kernel, dims),
        out_shape=jax.ShapeDtypeStruct((total, cols), F32),
        in_specs=[vmem] * 7,
        out_specs=vmem,
        scratch_shapes=[
            pltpu.VMEM((types, bins * low + last, LANES), BF16),
            pltpu.VMEM((types, last, LANES), F32),
            pltpu.VMEM((-(-collection.shape[2] // LANES), types * rows, LANES), F32),
            pltpu.VMEM((blocks * types * levels, rows, cols), F32),
            pltpu.VMEM((rows, 2 * cols), F32),
            pltpu.VMEM((types, rows, LANES), F32),
            pltpu.VMEM((types, rows, LANES), F32),
            pltpu.VMEM((rows, LANES), F32),
            pltpu.VMEM((rows, LANES), F32),
            pltpu.VMEM((rows, LANES), F32),
            pltpu.SemaphoreType.DMA((2,)),
            pltpu.SemaphoreType.DMA((2,)),
        ],
        compiler_params=pltpu.CompilerParams(
            collective_id=0, has_side_effects=True, vmem_limit_bytes=32 * 2**20
        ),
    )(
        spectra.reshape(total, cols),
        collection,
        growth_rate,
        fall_speed,
        supersaturation,
        courant,
        cloudy,
    )
    return out.reshape(spectra.shape)


def solution(mesh):
    return jax.shard_map(
        functools.partial(body, mesh.shape["gy"]),
        mesh=mesh,
        in_specs=(
            P("gx", None, None, None, "gy"),
            P(),
            P(),
            P(),
            P("gx", None, "gy"),
            P("gx", None, "gy"),
            P("gx", "gy"),
        ),
        out_specs=P("gx", None, None, None, "gy"),
        check_vma=False,
    )
```

```python
import functools

import jax
import jax.numpy as jnp
from jax import lax
from jax.experimental import pallas as pl
from jax.experimental.pallas import tpu as pltpu
from jax.sharding import PartitionSpec as P

SUB = 2
LANES = 128
CHUNK = 2
F32 = jnp.float32
BF16 = jnp.bfloat16


def rounded(x):
    return x.astype(BF16).astype(F32)


def kernel(
    dims,
    f_ref,
    coll_ref,
    rate_ref,
    fall_ref,
    sat_ref,
    cour_ref,
    cloudy_ref,
    out_ref,
    cm,
    k_last,
    raw,
    cells,
    gs,
    rates,
    falls,
    edge,
    from_left,
    from_right,
    send_sem,
    recv_sem,
):
    blocks, types, bins, levels, cols, n_y = dims
    low = bins // 8 * 8
    rows = low + 8
    per_type = blocks * levels
    groups = types * per_type
    me = lax.axis_index("gy")
    right, left = lax.rem(me + 1, n_y), lax.rem(me + n_y - 1, n_y)
    mesh_id = pl.DeviceIdType.MESH
    barrier = pltpu.get_barrier_semaphore()
    for peer in (left, right):
        pl.semaphore_signal(barrier, inc=1, device_id={"gy": peer}, device_id_type=mesh_id)

    lane = lax.broadcasted_iota(jnp.int32, (rows, LANES), 1)
    sub = lax.broadcasted_iota(jnp.int32, (rows, LANES), 0)

    def fill(t, packed):
        for b in range(blocks):
            for v in range(levels):
                g = (t * blocks + b) * levels + v
                base = ((b * types + t) * bins) * levels + v
                cells[g, bins:rows] = jnp.zeros((rows - bins, cols), F32)
                cells[g, 0:bins] = f_ref[pl.ds(base, bins, stride=levels), :]
                cells[g, bins : bins + 1] = cour_ref[b, v : v + 1, :]
                cells[g, bins + 1 : bins + 2] = sat_ref[b, v : v + 1, :]
                cells[g, bins + 2 : bins + 3] = cloudy_ref[b : b + 1, :].astype(F32)
                turned = pltpu.roll(cells[g], lax.rem(4 * g + 2, LANES), 1)
                packed = jnp.where((lane >= 4 * g) & (lane < 4 * g + 4), turned, packed)
        return packed

    packed = lax.fori_loop(0, types, fill, jnp.zeros((rows, LANES), F32))
    edge[...] = packed

    def column(ref, t):
        row = jnp.broadcast_to(ref[t : t + 1, :], (rows, bins))
        r = lax.broadcasted_iota(jnp.int32, (rows, bins), 0)
        c = lax.broadcasted_iota(jnp.int32, (rows, bins), 1)
        return jnp.sum(jnp.where(r == c, row, 0.0), axis=1, keepdims=True)

    for t in range(types):
        rates[t] = jnp.broadcast_to(column(rate_ref, t), (rows, LANES))
        falls[t] = jnp.broadcast_to(column(fall_ref, t), (rows, LANES))

    pairs = coll_ref.shape[2]
    raw[...] = jnp.zeros_like(raw)
    k_last[...] = jnp.zeros_like(k_last)
    sources = []
    for a in range(raw.shape[0]):
        width = min(LANES, pairs - a * LANES)
        for t in range(types):
            raw[a, t * rows : t * rows + bins, 0:width] = coll_ref[t, :, a * LANES : a * LANES + width]
        x = raw[a]
        hi = x.astype(BF16)
        sources.append(jnp.concatenate([hi, (x - hi.astype(F32)).astype(BF16)], axis=1))
    across = lax.broadcasted_iota(jnp.int32, (LANES, LANES), 1)
    down = lax.broadcasted_iota(jnp.int32, (LANES, LANES), 0)
    part, inner = across // rows, across % rows
    inner = jnp.where(inner < bins, inner, -1)
    inner_hi = jnp.where((part == 0) | (part == 2), inner, -1)
    inner_lo = jnp.where(part == 1, inner, -1)
    first = 0
    for i in range(bins):
        placed = None
        for a in range(first // LANES, (first + bins - i - 1) // LANES + 1):
            offset = first - i - a * LANES
            pick = jnp.concatenate(
                [
                    jnp.where((down == j + offset) & (j >= i), 1.0, 0.0).astype(BF16)
                    for j in (inner_hi, inner_lo)
                ],
                axis=0,
            )
            product = jnp.dot(sources[a], pick, preferred_element_type=F32)
            placed = product if placed is None else placed + product
        for t in range(types):
            cm[t, i * low : (i + 1) * low] = placed[t * rows : t * rows + low].astype(BF16)
            k_last[t, i : i + 1] = placed[t * rows + low : t * rows + bins]
        first += bins - i
    for t in range(types):
        cm[t, bins * low :] = k_last[t].astype(BF16)

    def column(ref, t):
        row = jnp.broadcast_to(ref[t : t + 1, :], (rows, bins))
        r = lax.broadcasted_iota(jnp.int32, (rows, bins), 0)
        c = lax.broadcasted_iota(jnp.int32, (rows, bins), 1)
        return jnp.sum(jnp.where(r == c, row, 0.0), axis=1, keepdims=True)

    for t in range(types):
        rates[t] = jnp.broadcast_to(column(rate_ref, t), (rows, LANES))
        falls[t] = jnp.broadcast_to(column(fall_ref, t), (rows, LANES))

    pairs = coll_ref.shape[2]
    raw[...] = jnp.zeros_like(raw)
    k_last[...] = jnp.zeros_like(k_last)
    sources = []
    for a in range(raw.shape[0]):
        width = min(LANES, pairs - a * LANES)
        for t in range(types):
            raw[a, t * rows : t * rows + bins, 0:width] = coll_ref[t, :, a * LANES : a * LANES + width]
        x = raw[a]
        hi = x.astype(BF16)
        sources.append(jnp.concatenate([hi, (x - hi.astype(F32)).astype(BF16)], axis=1))
    across = lax.broadcasted_iota(jnp.int32, (LANES, LANES), 1)
    down = lax.broadcasted_iota(jnp.int32, (LANES, LANES), 0)
    part, inner = across // rows, across % rows
    inner = jnp.where(inner < bins, inner, -1)
    inner_hi = jnp.where((part == 0) | (part == 2), inner, -1)
    inner_lo = jnp.where(part == 1, inner, -1)
    first = 0
    for i in range(bins):
        placed = None
        for a in range(first // LANES, (first + bins - i - 1) // LANES + 1):
            offset = first - i - a * LANES
            pick = jnp.concatenate(
                [
                    jnp.where((down == j + offset) & (j >= i), 1.0, 0.0).astype(BF16)
                    for j in (inner_hi, inner_lo)
                ],
                axis=0,
            )
            product = jnp.dot(sources[a], pick, preferred_element_type=F32)
            placed = product if placed is None else placed + product
        for t in range(types):
            cm[t, i * low : (i + 1) * low] = placed[t * rows : t * rows + low].astype(BF16)
            k_last[t, i : i + 1] = placed[t * rows + low : t * rows + bins]
        first += bins - i
    for t in range(types):
        cm[t, bins * low :] = k_last[t].astype(BF16)

    pl.semaphore_wait(barrier, 2)
    copies = []
    for index, (peer, landing) in enumerate(((right, from_left), (left, from_right))):
        copy = pltpu.make_async_remote_copy(
            src_ref=edge,
            dst_ref=landing,
            send_sem=send_sem.at[index],
            recv_sem=recv_sem.at[index],
            device_id={"gy": peer},
            device_id_type=mesh_id,
        )
        copy.start()
        copies.append(copy)

    def condense(f, r, sat):
        fr = r * f
        top = lax.broadcasted_iota(jnp.int32, f.shape, 0) < bins - 1
        up = jnp.where(top, fr, 0.0)
        rise = pltpu.roll(up, 1, 0) - up
        fall = pltpu.roll(fr, rows - 1, 0) - fr
        return f + jnp.maximum(sat, 0.0) * rise + jnp.maximum(-sat, 0.0) * fall

    def collide(t, g):
        width = g.shape[1]
        slot = gs.at[:, 0:width]
        slot[...] = g
        hi = rounded(g)
        stack = jnp.concatenate(
            [hi, hi, g - hi, jnp.zeros((LANES - 3 * rows, width), F32)], axis=0
        ).astype(BF16)
        acc = g[0:low]
        for start in range(0, bins, CHUNK):
            stop = min(start + CHUNK, bins)
            h = jnp.dot(cm[t, start * low : stop * low], stack, preferred_element_type=F32)
            for i in range(start, stop):
                acc = acc + slot[i : i + 1, :] * h[(i - start) * low : (i - start + 1) * low]
        h = jnp.dot(cm[t, bins * low :], stack, preferred_element_type=F32)
        last = jnp.sum(g * h[0:rows], axis=0, keepdims=True)
        rest = g[low:rows]
        rest = jnp.where(lax.broadcasted_iota(jnp.int32, rest.shape, 0) == 0, rest + last, rest)
        return jnp.concatenate([acc, rest], axis=0)

    def two(x, times):
        return jnp.concatenate([x] * times, axis=1) if times > 1 else x

    per = levels

    def one_block(at, carry):
        t, base = at // blocks, at * levels
        wet = []
        for v in range(0, levels, per):
            f = jnp.concatenate([cells[base + v + p] for p in range(per)], axis=1)
            g = condense(f, two(rates[t], per), f[bins + 1 : bins + 2])
            for _ in range(SUB):
                g = collide(t, g)
            w = jnp.where(f[bins + 2 : bins + 3] > 0, g, f)
            wet += [w[:, p * LANES : (p + 1) * LANES] for p in range(per)]
        for v in range(levels):
            above = wet[v + 1] if v + 1 < levels else jnp.zeros_like(wet[v])
            cells[base + v] = wet[v] + falls[t] * (above - wet[v])
        return carry

    early = types * blocks // 4
    lax.fori_loop(0, early, one_block, 0)
    lax.fori_loop(early, types * blocks, one_block, 0)

    for copy in copies:
        copy.wait()
    f = jnp.where(lane % 4 < 2, from_left[...], from_right[...])
    kind = lane // (4 * per_type)
    r, v_fall = rates[0], falls[0]
    for t in range(1, types):
        r = jnp.where(kind == t, rates[t], r)
        v_fall = jnp.where(kind == t, falls[t], v_fall)
    g = condense(f, r, f[bins + 1 : bins + 2])

    def one_type(t, new):
        mine = g
        for _ in range(SUB):
            mine = collide(t, mine)
        return jnp.where(kind == t, mine, new)

    g = lax.fori_loop(0, types, one_type, g, unroll=True)
    w = jnp.where(f[bins + 2 : bins + 3] > 0, g, f)
    above = jnp.where(lane // 4 % levels == levels - 1, 0.0, pltpu.roll(w, LANES - 4, 1))
    ghost = w + v_fall * (above - w)
    edge[...] = ghost

    def shifted(g, x, width_lane):
        near = pltpu.roll(edge[...], lax.rem(cols + LANES - 2 - 4 * g, LANES), 1)
        m2 = pltpu.roll(jnp.where(width_lane >= cols - 2, near, x), 2, 1)
        m1 = pltpu.roll(jnp.where(width_lane == cols - 1, near, x), 1, 1)
        p1 = pltpu.roll(jnp.where(width_lane == 0, near, x), LANES - 1, 1)
        p2 = pltpu.roll(jnp.where(width_lane < 2, near, x), LANES - 2, 1)
        return m2, m1, p1, p2

    def advect(at, carry):
        b, v = at // levels, lax.rem(at, levels)
        coef = None
        for t in range(types):
            g = (t * blocks + b) * levels + v
            x = cells[g]
            m2, m1, p1, p2 = shifted(g, x, lane)
            if coef is None:
                c = 0.5 * (x[bins : bins + 1] + p1[bins : bins + 1])
                d = 0.5 * (x[bins : bins + 1] + m1[bins : bins + 1])
                ca, da = jnp.abs(c), jnp.abs(d)
                coef = [
                    jnp.broadcast_to(e * (1.0 / 12.0), (rows, LANES))
                    for e in (
                        da - d,
                        7.0 * d - 3.0 * da - (ca - c),
                        7.0 * d + 3.0 * da - (7.0 * c - 3.0 * ca),
                        -d - da - (7.0 * c + 3.0 * ca),
                        c + ca,
                    )
                ]
            y = x + coef[2] * x + coef[0] * m2 + coef[1] * m1 + coef[3] * p1 + coef[4] * p2
            base = ((b * types + t) * bins) * levels + v
            out_ref[pl.ds(base, bins, stride=levels), :] = y[0:bins]
        return carry

    lax.fori_loop(0, per_type, advect, 0)


def body(n_y, spectra, collection, growth_rate, fall_speed, supersaturation, courant, cloudy):
    blocks, types, bins, levels, cols = spectra.shape
    dims = (blocks, types, bins, levels, cols, n_y)
    low = bins // 8 * 8
    rows = low + 8
    total = blocks * types * bins * levels
    last = -(-rows // 16) * 16
    vmem = pl.BlockSpec(memory_space=pltpu.VMEM)
    out = pl.pallas_call(
        functools.partial(kernel, dims),
        out_shape=jax.ShapeDtypeStruct((total, cols), F32),
        in_specs=[vmem] * 7,
        out_specs=vmem,
        scratch_shapes=[
            pltpu.VMEM((types, bins * low + last, LANES), BF16),
            pltpu.VMEM((types, last, LANES), F32),
            pltpu.VMEM((-(-collection.shape[2] // LANES), types * rows, LANES), F32),
            pltpu.VMEM((blocks * types * levels, rows, cols), F32),
            pltpu.VMEM((rows, 4 * cols), F32),
            pltpu.VMEM((types, rows, LANES), F32),
            pltpu.VMEM((types, rows, LANES), F32),
            pltpu.VMEM((rows, LANES), F32),
            pltpu.VMEM((rows, LANES), F32),
            pltpu.VMEM((rows, LANES), F32),
            pltpu.SemaphoreType.DMA((2,)),
            pltpu.SemaphoreType.DMA((2,)),
        ],
        compiler_params=pltpu.CompilerParams(
            collective_id=0, has_side_effects=True, vmem_limit_bytes=32 * 2**20
        ),
    )(
        spectra.reshape(total, cols),
        collection,
        growth_rate,
        fall_speed,
        supersaturation,
        courant,
        cloudy,
    )
    return out.reshape(spectra.shape)


def solution(mesh):
    return jax.shard_map(
        functools.partial(body, mesh.shape["gy"]),
        mesh=mesh,
        in_specs=(
            P("gx", None, None, None, "gy"),
            P(),
            P(),
            P(),
            P("gx", None, "gy"),
            P("gx", None, "gy"),
            P("gx", "gy"),
        ),
        out_specs=P("gx", None, None, None, "gy"),
        check_vma=False,
    )
```
